32 devices in a mesh: rep: 1, tp: 16 (over z, y, x), sub: 2 (over core).
Axes of the slice: x: 2, y: 2, z: 4, core: 2. Of those that a mesh axis runs over, the one named last changes fastest.
Arguments:
- tokens: bfloat16 [256, 8192], P(('rep', 'tp'), 'sub'), may hold values from -6 to 6
- gate_projection_weight: bfloat16 [8192, 28672], P('sub', 'tp'), may hold values from -0.0625 to 0.0625
- up_projection_weight: bfloat16 [8192, 28672], P('sub', 'tp'), may hold values from -0.0625 to 0.0625
- down_projection_weight: bfloat16 [28672, 8192], P('tp', 'sub'), may hold values from -0.03125 to 0.03125
- adapter_down_store: bfloat16 [64, 64, 8192], P('tp', None, 'sub'), may hold values from -0.0625 to 0.0625
- adapter_up_store: bfloat16 [64, 64, 8192], P('tp', None, 'sub'), may hold values from -0.75 to 0.75
- request_adapter_index: int32 [256], P('rep'), may hold values from 0 to 63, never falling along the last dimension, each value on 1 to 32 neighbouring positions
- adapter_store_row: int32 [64], replicated, may hold values from 0 to 63, each once
Outputs:
- mixed: bfloat16 [256, 8192], P(('rep', 'tp'), 'sub')
The draws below stay inside these ranges and needn't reach their ends.
Inputs may be any that keep to these rules, and one draw needn't show every extreme that they name: `request_adapter_index`: never falling; each of the 64 adapters is named by 1 to 32 consecutive requests, one adapter by exactly 32. A permutation: the panels of adapter a are row adapter_store_row[a] of adapter_down_store and adapter_up_store.
All inputs are finite; a program needn't handle non-finite values.
Results may differ from the reference program's by a relative error of at most 0.0051.
Values may be sent and summed in bfloat16 or wider, within the bound.
A program may use at most 192 MiB of HBM per device.

```python
import math
import jax
import jax.numpy as jnp
import numpy as np
from jax import lax

MODEL_WIDTH = 8192
FF = 28672
ADAPTER_RANK = 64
ROWS = 256
ADAPTER_COUNT = 64
MOST = 32


def block_scale(own_key, dims, cuts, smallest, top_value):
    def one(position, blocks):
        draws = jax.random.uniform(jax.random.fold_in(jax.random.fold_in(own_key, 6), position), (blocks,), jnp.float32, smallest / len(cuts), top_value / len(cuts))
        return jnp.repeat(jnp.exp(draws), dims[position] // blocks).reshape((-1,) + (1,) * (len(dims) - position - 1))

    gain = one(*cuts[0])
    for cut in cuts[1:]:
        gain = gain * one(*cut)
    return gain


def profile(number_of, total, reach, skew):
    loads = [(1 << 20) // math.isqrt(standing ** skew) + 1 for standing in range(2, number_of + 1)]
    rest, counts = total - reach - (number_of - 1), [1] * (number_of - 1)
    while rest > 0:
        free = [i for i in range(number_of - 1) if counts[i] < reach]
        whole, remaining = sum([loads[i] for i in free]), rest
        for i in free:
            addition = min(reach - counts[i], max(1, remaining * loads[i] // whole), rest)
            counts[i] = counts[i] + addition
            rest = rest - addition
    return np.array([reach] + counts)


def ragged_sizes(key, amount, total, limit, lean):
    if amount == 2:
        one = jax.random.randint(key, (), max(1, total - limit), min(limit, total - 1) + 1)
        return jnp.stack([one, total - one])
    lengths = jnp.asarray(profile(amount, total, limit, lean), jnp.int32)
    twos = (amount - 1) // 2
    source_of, taker = lengths[1:1 + 2 * twos:2], lengths[2:2 + 2 * twos:2]
    margin = jnp.minimum(source_of - 1, limit - taker)
    moved = jax.random.randint(jax.random.fold_in(key, 1), (twos,), 0, 1 << 20) % (margin + 1)
    lengths = lengths.at[1:1 + 2 * twos:2].set(source_of - moved).at[2:2 + 2 * twos:2].set(taker + moved)
    return lengths[jax.random.permutation(jax.random.fold_in(key, 2), amount)]


def centred(key, dims, deviation, limit, cuts=(), held_as=jnp.bfloat16):
    result = deviation * jax.random.normal(key, dims, jnp.float32)
    if cuts:
        result = result * block_scale(key, dims, cuts, -0.22, 0.18)
    return jnp.clip(result, -limit, limit).astype(held_as)


def setup_inputs(seed: int = 0, part: int = 0) -> dict:
    key_of = jax.random.split(jax.random.key(seed), 9)
    part_keys = jax.random.split(jax.random.fold_in(key_of[8], part), 9)
    return {
        "tokens": centred(part_keys[0], (ROWS, MODEL_WIDTH), 1.0, 6.0, ((0, 16), (1, 2))),
        "gate_projection_weight": centred(key_of[1], (MODEL_WIDTH, FF), MODEL_WIDTH ** -0.5, 0.0625, ((0, 2), (1, 16))),
        "up_projection_weight": centred(key_of[2], (MODEL_WIDTH, FF), MODEL_WIDTH ** -0.5, 0.0625, ((0, 2), (1, 16))),
        "down_projection_weight": centred(key_of[3], (FF, MODEL_WIDTH), FF ** -0.5, 0.03125, ((0, 16), (1, 2))),
        "adapter_down_store": centred(key_of[4], (ADAPTER_COUNT, ADAPTER_RANK, MODEL_WIDTH), MODEL_WIDTH ** -0.5, 0.0625, ((0, 16), (2, 2))),
        "adapter_up_store": centred(key_of[5], (ADAPTER_COUNT, ADAPTER_RANK, MODEL_WIDTH), ADAPTER_RANK ** -0.5, 0.75, ((0, 16), (2, 2))),
        "request_adapter_index": jnp.searchsorted(jnp.cumsum(ragged_sizes(part_keys[6], ADAPTER_COUNT, ROWS, MOST, 2)), jnp.arange(ROWS), side="right").astype(jnp.int32),
        "adapter_store_row": jax.random.permutation(key_of[7], ADAPTER_COUNT).astype(jnp.int32),
    }


def reference(tokens, gate_projection_weight, up_projection_weight, down_projection_weight, adapter_down_store, adapter_up_store, request_adapter_index, adapter_store_row):
    gate = jnp.dot(tokens, gate_projection_weight, preferred_element_type=jnp.float32)
    up = jnp.dot(tokens, up_projection_weight, preferred_element_type=jnp.float32)
    hidden = (jax.nn.silu(gate) * up).astype(jnp.bfloat16)
    base = jnp.dot(hidden, down_projection_weight, preferred_element_type=jnp.float32)
    row_slots = adapter_store_row[request_adapter_index].astype(jnp.int32)

    def one_request(packed):
        request_row_input, store_row_number = packed
        rank_activation = jnp.dot(adapter_down_store[store_row_number], request_row_input, preferred_element_type=jnp.float32).astype(jnp.bfloat16)
        return jnp.dot(rank_activation, adapter_up_store[store_row_number], preferred_element_type=jnp.float32)

    adapted = lax.map(one_request, (tokens, row_slots))
    return (base + adapted).astype(jnp.bfloat16)
```

```python
import jax
import jax.numpy as jnp
from jax import lax
from jax.experimental import pallas as pl
from jax.experimental.pallas import tpu as pltpu
from jax.sharding import PartitionSpec as P

MESH = pl.DeviceIdType.MESH
ZS = 4
STEPS = 8
SLOTS = 6
PARTS = 8
TILE = 256


def plain(
    tokens,
    gate_projection_weight,
    up_projection_weight,
    down_projection_weight,
    adapter_down_store,
    adapter_up_store,
    request_adapter_index,
    adapter_store_row,
):
    every_row = lax.all_gather(tokens, "tp", axis=0, tiled=True)
    batch_row_count = every_row.shape[0]
    row_span = batch_row_count // 8
    local_store_rows = adapter_down_store.shape[0]
    tp_place = lax.axis_index("tp")
    numbers = jnp.arange(adapter_store_row.shape[0], dtype=jnp.int32)
    gate_part = jnp.dot(every_row, gate_projection_weight, preferred_element_type=jnp.float32)
    up_part = jnp.dot(every_row, up_projection_weight, preferred_element_type=jnp.float32)
    begins = []
    members = []
    low_list = []
    for store_row_index in range(local_store_rows):
        target = tp_place * local_store_rows + store_row_index
        adapter = jnp.sum(jnp.where(adapter_store_row == target, numbers, 0))
        offset = jnp.sum((request_adapter_index < adapter).astype(jnp.int32))
        row_begin = jnp.minimum(offset, batch_row_count - row_span)
        row_block = lax.dynamic_slice_in_dim(every_row, row_begin, row_span, 0)
        member = lax.dynamic_slice_in_dim(request_adapter_index, row_begin, row_span, 0) == adapter
        low_list.append(
            lax.dot_general(
                row_block,
                adapter_down_store[store_row_index],
                (((1,), (1,)), ((), ())),
                preferred_element_type=jnp.float32,
            )
        )
        begins.append(row_begin)
        members.append(member)
    low_parts = jnp.stack(low_list)
    gate_sum, up_sum, low_sum = lax.psum((gate_part, up_part, low_parts), "sub")
    hidden = (jax.nn.silu(gate_sum) * up_sum).astype(jnp.bfloat16)
    rank_activation = low_sum.astype(jnp.bfloat16)
    adapter_output = jnp.zeros((batch_row_count, adapter_up_store.shape[2]), jnp.float32)
    for store_row_index in range(local_store_rows):
        product = jnp.dot(
            rank_activation[store_row_index],
            adapter_up_store[store_row_index],
            preferred_element_type=jnp.float32,
        )
        product = jnp.where(members[store_row_index][:, None], product, 0.0)
        current = lax.dynamic_slice_in_dim(adapter_output, begins[store_row_index], row_span, 0)
        adapter_output = lax.dynamic_update_slice_in_dim(
            adapter_output, current + product, begins[store_row_index], 0
        )
    base_rows = jnp.dot(hidden, down_projection_weight, preferred_element_type=jnp.float32)
    summed = lax.psum_scatter(base_rows + adapter_output, "tp", scatter_dimension=0, tiled=True)
    return summed.astype(jnp.bfloat16)


def layer_kernel(
    tokens_ref, gate_hbm, up_hbm, down_hbm, adown_hbm, aup_hbm, index_ref, store_ref,
    out_ref,
    tok, wg, wu, wa, wd, acc, low, from_core, low_from_core, hid, base,
    send1, recv1, send2, recv2, send3, recv3, index_rel,
    w_sem, d_sem, z_send, z_recv, n_send, n_recv, e_send, e_recv, h_send, h_recv,
    r_send, r_recv, rz_send, rz_recv,
):
    tp = lax.axis_index("tp")
    sub = lax.axis_index("sub")
    rep = lax.axis_index("rep")
    rows = tok.shape[1]
    own = tokens_ref.shape[0]
    group = ZS * own
    width = tok.shape[2]
    tiles = acc.shape[0]
    columns = base.shape[2]
    half = rows // 2

    x = tp % 2
    y = (tp // 2) % 2
    z = tp // 4
    flips = (z, z + 1 - 2 * (z % 2), z + 2 - 4 * (z // 2), 3 - z)
    crosses = (0, 1 - 2 * x, 2 - 4 * y, 3 - 2 * (x + 2 * y))

    def place(q, k):
        return flips[k] * 4 + x + 2 * y + crosses[q]

    z_peers = [(rep, flips[k] * 4 + x + 2 * y, sub) for k in range(1, ZS)]
    first = (rep, tp + crosses[1] * (1 - sub) + crosses[2] * sub, sub)
    second = (rep, tp + crosses[2] * (1 - sub) + crosses[1] * sub, sub)
    first_rows = pl.ds(pl.multiple_of((1 + sub) * group, group), group)
    second_rows = pl.ds(pl.multiple_of((2 - sub) * group, group), group)
    own_rows = pl.ds(0, group)
    cross_rows = pl.ds(3 * group, group)
    core = (rep, tp, 1 - sub)
    my_half = pl.ds(pl.multiple_of(sub * half, half), half)
    core_half = pl.ds(pl.multiple_of((1 - sub) * half, half), half)

    def weight_copies(c):
        slot = c % SLOTS
        part = pl.ds(pl.multiple_of(c * width, width), width)
        return (
            pltpu.make_async_copy(gate_hbm.at[part, :], wg.at[slot], w_sem.at[0, slot]),
            pltpu.make_async_copy(up_hbm.at[part, :], wu.at[slot], w_sem.at[1, slot]),
            pltpu.make_async_copy(adown_hbm.at[:, part], wa.at[slot], w_sem.at[2, slot]),
        )

    hidden_units = down_hbm.shape[0]
    down_copies = (
        pltpu.make_async_copy(down_hbm, wd.at[pl.ds(0, hidden_units), :], d_sem.at[0]),
        pltpu.make_async_copy(
            aup_hbm, wd.at[pl.ds(hidden_units, aup_hbm.shape[0]), :], d_sem.at[1]
        ),
    )

    def remote(source, target, sent, received, device):
        return pltpu.make_async_remote_copy(
            src_ref=source, dst_ref=target, send_sem=sent, recv_sem=received,
            device_id=device, device_id_type=MESH,
        )

    def z_copy(c, k):
        return remote(
            tok.at[c, pl.ds(0, own), :], tok.at[c, pl.ds(k * own, own), :],
            z_send.at[c, k - 1], z_recv.at[c, k - 1], z_peers[k - 1],
        )

    def near_copies(c):
        return (
            remote(tok.at[c, own_rows, :], tok.at[c, first_rows, :],
                   n_send.at[0, c], n_recv.at[0, c], first),
            remote(tok.at[c, own_rows, :], tok.at[c, second_rows, :],
                   n_send.at[1, c], n_recv.at[1, c], second),
        )

    def cross_copy(c):
        return remote(tok.at[c, first_rows, :], tok.at[c, cross_rows, :],
                      n_send.at[2, c], n_recv.at[2, c], second)

    def core_copy(j):
        return remote(acc.at[j, core_half, :], from_core.at[j], e_send.at[j], e_recv.at[j], core)

    low_copy = remote(low.at[core_half, :], low_from_core, e_send.at[tiles], e_recv.at[tiles], core)

    def hidden_copy(j):
        block = hid.at[my_half, pl.ds(pl.multiple_of(j * TILE, TILE), TILE)]
        return remote(block, block, h_send.at[j], h_recv.at[j], core)

    def sum_copy1(n):
        return remote(send1.at[n], recv1.at[n], r_send.at[0, n], r_recv.at[0, n], second)

    def sum_copy2(n):
        return remote(send2.at[n], recv2.at[n], r_send.at[1, n], r_recv.at[1, n], first)

    def sum_copy3(n, k):
        return remote(send3.at[n, k - 1], recv3.at[n, k - 1],
                      rz_send.at[n, k - 1], rz_recv.at[n, k - 1], z_peers[k - 1])

    barrier = pltpu.get_barrier_semaphore()
    peers = z_peers + [first, second, core]
    for peer in peers:
        pl.semaphore_signal(barrier, inc=1, device_id=peer, device_id_type=MESH)
    for c in range(SLOTS):
        for copy in weight_copies(c):
            copy.start()
    for copy in down_copies:
        copy.start()
    for c in range(STEPS):
        tok[c, 0:own, :] = tokens_ref[:, c * width:(c + 1) * width]
    pl.semaphore_wait(barrier, len(peers))
    for c in range(STEPS):
        for k in range(1, ZS):
            z_copy(c, k).start()

    @pl.loop(0, tiles)
    def _(j):
        acc[j] = jnp.zeros(acc.shape[1:], jnp.float32)

    low[...] = jnp.zeros_like(low)
    for q in range(4):
        for k in range(ZS):
            source = pl.ds(pl.multiple_of(place(q, k) * own, own), own)
            index_rel[pl.ds(q * group + k * own, own), :] = index_ref[source, :]

    def gather_step(t, carry):
        @pl.when(t < STEPS)
        def _():
            for k in range(1, ZS):
                z_copy(t, k).wait_recv()
            for copy in near_copies(t):
                copy.start()

        @pl.when((t >= 1) & (t < STEPS + 1))
        def _():
            near_copies(t - 1)[0].wait_recv()
            cross_copy(t - 1).start()

        @pl.when(t >= 2)
        def _():
            c = t - 2
            slot = c % SLOTS
            near_copies(c)[1].wait_recv()
            cross_copy(c).wait_recv()
            for copy in weight_copies(c):
                copy.wait()

            @pl.loop(0, tiles)
            def _(j):
                part = pl.ds(pl.multiple_of(j * TILE, TILE), TILE)
                acc[j, :, 0:TILE] += jnp.dot(
                    tok[c], wg[slot, :, part], preferred_element_type=jnp.float32
                )
                acc[j, :, TILE:2 * TILE] += jnp.dot(
                    tok[c], wu[slot, :, part], preferred_element_type=jnp.float32
                )

                @pl.when(c == STEPS - 1)
                def _():
                    core_copy(j).start()

            low[...] += lax.dot_general(
                tok[c], wa[slot], (((1,), (1,)), ((), ())), preferred_element_type=jnp.float32
            )

            @pl.when(c + SLOTS < STEPS)
            def _():
                for copy in weight_copies(c + SLOTS):
                    copy.start()

        return carry

    lax.fori_loop(0, STEPS + 2, gather_step, 0)
    low_copy.start()

    @pl.loop(0, tiles)
    def _(j):
        core_copy(j).wait_recv()
        gate = acc[j, my_half, 0:TILE] + from_core[j, :, 0:TILE]
        up = acc[j, my_half, TILE:2 * TILE] + from_core[j, :, TILE:2 * TILE]
        value = gate / (1.0 + jnp.exp(-gate)) * up
        hid[my_half, pl.ds(pl.multiple_of(j * TILE, TILE), TILE)] = value.astype(jnp.bfloat16)
        hidden_copy(j).start()

    low_copy.wait_recv()
    adapters = store_ref.shape[1]
    ranks = low.shape[1]
    local = ranks // 64
    numbers = lax.broadcasted_iota(jnp.int32, (half, adapters), 1)
    store = jnp.broadcast_to(store_ref[...].astype(jnp.float32), (half, adapters))
    row_of = jnp.sum(
        jnp.where(index_rel[my_half, :] == numbers, store, 0.0), axis=1, keepdims=True
    )
    held = lax.broadcasted_iota(jnp.int32, (half, ranks), 1) // 64 + tp * local
    low_sum = low[my_half, :] + low_from_core[...]
    low_sum = jnp.where(row_of == held.astype(jnp.float32), low_sum, 0.0)
    hid[my_half, pl.ds(tiles * TILE, TILE)] = low_sum.astype(jnp.bfloat16)
    hidden_copy(tiles).start()
    for copy in down_copies:
        copy.wait()

    @pl.loop(0, tiles + 1)
    def _(j):
        hidden_copy(j).wait_recv()

    def sum_step(t, carry):
        @pl.when(t < PARTS)
        def _():
            @pl.loop(0, columns // TILE)
            def _(i):
                part = pl.ds(pl.multiple_of(i * TILE, TILE), TILE)
                whole = pl.ds(pl.multiple_of(t * columns + i * TILE, TILE), TILE)
                base[t, :, part] = jnp.dot(
                    hid[...], wd[:, whole], preferred_element_type=jnp.float32
                )

            send1[t, 0:group, :] = base[t, second_rows, :].astype(jnp.bfloat16)
            send1[t, group:2 * group, :] = base[t, cross_rows, :].astype(jnp.bfloat16)
            sum_copy1(t).start()

        @pl.when((t >= 2) & (t < PARTS + 2))
        def _():
            n = t - 2
            sum_copy1(n).wait_recv()
            send2[n] = (
                base[n, first_rows, :] + recv1[n, group:2 * group, :].astype(jnp.float32)
            ).astype(jnp.bfloat16)
            sum_copy2(n).start()
            base[n, own_rows, :] += recv1[n, 0:group, :].astype(jnp.float32)

        @pl.when((t >= 3) & (t < PARTS + 3))
        def _():
            n = t - 3
            sum_copy2(n).wait_recv()
            total = base[n, own_rows, :] + recv2[n].astype(jnp.float32)
            base[n, pl.ds(0, own), :] = total[0:own]
            for k in range(1, ZS):
                send3[n, k - 1] = total[k * own:(k + 1) * own].astype(jnp.bfloat16)
                sum_copy3(n, k).start()

        @pl.when(t >= 4)
        def _():
            n = t - 4
            total = base[n, pl.ds(0, own), :]
            for k in range(1, ZS):
                sum_copy3(n, k).wait_recv()
                total += recv3[n, k - 1].astype(jnp.float32)
            whole = pl.ds(pl.multiple_of(n * columns, columns), columns)
            out_ref[:, whole] = total.astype(jnp.bfloat16)

        return carry

    lax.fori_loop(0, PARTS + 4, sum_step, 0)

    @pl.loop(0, STEPS)
    def _(c):
        for k in range(1, ZS):
            z_copy(c, k).wait_send()
        for copy in near_copies(c):
            copy.wait_send()
        cross_copy(c).wait_send()

    @pl.loop(0, tiles)
    def _(j):
        core_copy(j).wait_send()

    low_copy.wait_send()

    @pl.loop(0, tiles + 1)
    def _(j):
        hidden_copy(j).wait_send()

    @pl.loop(0, PARTS)
    def _(n):
        sum_copy1(n).wait_send()
        sum_copy2(n).wait_send()
        for k in range(1, ZS):
            sum_copy3(n, k).wait_send()


def fused(
    tokens,
    gate_projection_weight,
    up_projection_weight,
    down_projection_weight,
    adapter_down_store,
    adapter_up_store,
    request_adapter_index,
    adapter_store_row,
):
    own, features = tokens.shape
    rows = request_adapter_index.shape[0]
    units = gate_projection_weight.shape[1]
    held, rank, _ = adapter_down_store.shape
    ranks = held * rank
    width = features // STEPS
    columns = features // PARTS
    tiles = units // TILE
    group = ZS * own
    bf16, f32 = jnp.bfloat16, jnp.float32
    dma = pltpu.SemaphoreType.DMA
    vmem = pl.BlockSpec(memory_space=pltpu.VMEM)
    hbm = pl.BlockSpec(memory_space=pl.ANY)
    return pl.pallas_call(
        layer_kernel,
        out_shape=jax.ShapeDtypeStruct((own, features), bf16),
        in_specs=[vmem, hbm, hbm, hbm, hbm, hbm, vmem, vmem],
        out_specs=vmem,
        scratch_shapes=[
            pltpu.VMEM((STEPS, rows, width), bf16),
            pltpu.VMEM((SLOTS, width, units), bf16),
            pltpu.VMEM((SLOTS, width, units), bf16),
            pltpu.VMEM((SLOTS, ranks, width), bf16),
            pltpu.VMEM((units + ranks, features), bf16),
            pltpu.VMEM((tiles, rows, 2 * TILE), f32),
            pltpu.VMEM((rows, ranks), f32),
            pltpu.VMEM((tiles, rows // 2, 2 * TILE), f32),
            pltpu.VMEM((rows // 2, ranks), f32),
            pltpu.VMEM((rows, units + ranks), bf16),
            pltpu.VMEM((PARTS, rows, columns), f32),
            pltpu.VMEM((PARTS, 2 * group, columns), bf16),
            pltpu.VMEM((PARTS, 2 * group, columns), bf16),
            pltpu.VMEM((PARTS, group, columns), bf16),
            pltpu.VMEM((PARTS, group, columns), bf16),
            pltpu.VMEM((PARTS, ZS - 1, own, columns), bf16),
            pltpu.VMEM((PARTS, ZS - 1, own, columns), bf16),
            pltpu.VMEM((rows, 1), jnp.int32),
            dma((3, SLOTS)),
            dma((2,)),
            dma((STEPS, ZS - 1)),
            dma((STEPS, ZS - 1)),
            dma((3, STEPS)),
            dma((3, STEPS)),
            dma((tiles + 1,)),
            dma((tiles + 1,)),
            dma((tiles + 1,)),
            dma((tiles + 1,)),
            dma((2, PARTS)),
            dma((2, PARTS)),
            dma((PARTS, ZS - 1)),
            dma((PARTS, ZS - 1)),
        ],
        compiler_params=pltpu.CompilerParams(
            collective_id=0, has_side_effects=True, vmem_limit_bytes=61 * 1024 * 1024
        ),
    )(
        tokens,
        gate_projection_weight,
        up_projection_weight,
        down_projection_weight,
        adapter_down_store.reshape(ranks, features),
        adapter_up_store.reshape(ranks, features),
        request_adapter_index.reshape(rows, 1),
        adapter_store_row.reshape(1, adapter_store_row.shape[0]),
    )


def solution(mesh):
    small = mesh.shape["tp"] == 16 and mesh.shape["rep"] == 1
    return jax.shard_map(
        fused if small else plain,
        mesh=mesh,
        in_specs=(
            P(("rep", "tp"), "sub"),
            P("sub", "tp"),
            P("sub", "tp"),
            P("tp", "sub"),
            P("tp", None, "sub"),
            P("tp", None, "sub"),
            P("rep"),
            P(),
        ),
        out_specs=P(("rep", "tp"), "sub"),
        check_vma=False,
    )
```

```python
import jax
import jax.numpy as jnp
from jax import lax
from jax.experimental import pallas as pl
from jax.experimental.pallas import tpu as pltpu
from jax.sharding import PartitionSpec as P

MESH = pl.DeviceIdType.MESH
ZS = 4
STEPS = 4
SLOTS = 3
PARTS = 8
TILE = 256
GATHER_LAGS = (1, 3)
SUM_LAGS = (2, 4, 6)


def plain(
    tokens,
    gate_projection_weight,
    up_projection_weight,
    down_projection_weight,
    adapter_down_store,
    adapter_up_store,
    request_adapter_index,
    adapter_store_row,
):
    every_row = lax.all_gather(tokens, "tp", axis=0, tiled=True)
    batch_row_count = every_row.shape[0]
    row_span = batch_row_count // 8
    local_store_rows = adapter_down_store.shape[0]
    tp_place = lax.axis_index("tp")
    numbers = jnp.arange(adapter_store_row.shape[0], dtype=jnp.int32)
    gate_part = jnp.dot(every_row, gate_projection_weight, preferred_element_type=jnp.float32)
    up_part = jnp.dot(every_row, up_projection_weight, preferred_element_type=jnp.float32)
    begins = []
    members = []
    low_list = []
    for store_row_index in range(local_store_rows):
        target = tp_place * local_store_rows + store_row_index
        adapter = jnp.sum(jnp.where(adapter_store_row == target, numbers, 0))
        offset = jnp.sum((request_adapter_index < adapter).astype(jnp.int32))
        row_begin = jnp.minimum(offset, batch_row_count - row_span)
        row_block = lax.dynamic_slice_in_dim(every_row, row_begin, row_span, 0)
        member = lax.dynamic_slice_in_dim(request_adapter_index, row_begin, row_span, 0) == adapter
        low_list.append(
            lax.dot_general(
                row_block,
                adapter_down_store[store_row_index],
                (((1,), (1,)), ((), ())),
                preferred_element_type=jnp.float32,
            )
        )
        begins.append(row_begin)
        members.append(member)
    low_parts = jnp.stack(low_list)
    gate_sum, up_sum, low_sum = lax.psum((gate_part, up_part, low_parts), "sub")
    hidden = (jax.nn.silu(gate_sum) * up_sum).astype(jnp.bfloat16)
    rank_activation = low_sum.astype(jnp.bfloat16)
    adapter_output = jnp.zeros((batch_row_count, adapter_up_store.shape[2]), jnp.float32)
    for store_row_index in range(local_store_rows):
        product = jnp.dot(
            rank_activation[store_row_index],
            adapter_up_store[store_row_index],
            preferred_element_type=jnp.float32,
        )
        product = jnp.where(members[store_row_index][:, None], product, 0.0)
        current = lax.dynamic_slice_in_dim(adapter_output, begins[store_row_index], row_span, 0)
        adapter_output = lax.dynamic_update_slice_in_dim(
            adapter_output, current + product, begins[store_row_index], 0
        )
    base_rows = jnp.dot(hidden, down_projection_weight, preferred_element_type=jnp.float32)
    summed = lax.psum_scatter(base_rows + adapter_output, "tp", scatter_dimension=0, tiled=True)
    return summed.astype(jnp.bfloat16)


def layer_kernel(
    tokens_ref, gate_hbm, up_hbm, down_hbm, adown_hbm, aup_hbm, index_ref, store_ref,
    out_ref,
    tok, wg, wu, wa, wd, acc, low, from_core, low_from_core, hid, base,
    send1, recv1, send2, recv2, send3, recv3, index_all, index_rel,
    w_sem, d_sem, z_send, z_recv, n_send, n_recv, e_send, e_recv, h_send, h_recv,
    r_send, r_recv, rz_send, rz_recv,
):
    tp = lax.axis_index("tp")
    sub = lax.axis_index("sub")
    rep = lax.axis_index("rep")
    rows = tok.shape[1]
    own = tokens_ref.shape[0]
    group = ZS * own
    width = tok.shape[2]
    tiles = acc.shape[0]
    columns = base.shape[2]
    half = rows // 2

    x = tp % 2
    y = (tp // 2) % 2
    z = tp // 4
    flips = (z, z + 1 - 2 * (z % 2), z + 2 - 4 * (z // 2), 3 - z)
    crosses = (0, 1 - 2 * x, 2 - 4 * y, 3 - 2 * (x + 2 * y))

    def place(q, k):
        return flips[k] * 4 + x + 2 * y + crosses[q]

    z_peers = [(rep, flips[k] * 4 + x + 2 * y, sub) for k in range(1, ZS)]
    first = (rep, tp + crosses[1] * (1 - sub) + crosses[2] * sub, sub)
    second = (rep, tp + crosses[2] * (1 - sub) + crosses[1] * sub, sub)
    first_rows = pl.ds(pl.multiple_of((1 + sub) * group, group), group)
    second_rows = pl.ds(pl.multiple_of((2 - sub) * group, group), group)
    own_rows = pl.ds(0, group)
    cross_rows = pl.ds(3 * group, group)
    core = (rep, tp, 1 - sub)
    my_half = pl.ds(pl.multiple_of(sub * half, half), half)
    core_half = pl.ds(pl.multiple_of((1 - sub) * half, half), half)

    def weight_copies(c):
        slot = c % SLOTS
        part = pl.ds(pl.multiple_of(c * width, width), width)
        return (
            pltpu.make_async_copy(gate_hbm.at[part, :], wg.at[slot], w_sem.at[0, slot]),
            pltpu.make_async_copy(up_hbm.at[part, :], wu.at[slot], w_sem.at[1, slot]),
            pltpu.make_async_copy(adown_hbm.at[:, part], wa.at[slot], w_sem.at[2, slot]),
        )

    hidden_units = down_hbm.shape[0]
    down_copies = (
        pltpu.make_async_copy(down_hbm, wd.at[pl.ds(0, hidden_units), :], d_sem.at[0]),
        pltpu.make_async_copy(
            aup_hbm, wd.at[pl.ds(hidden_units, aup_hbm.shape[0]), :], d_sem.at[1]
        ),
    )

    def remote(source, target, sent, received, device):
        return pltpu.make_async_remote_copy(
            src_ref=source, dst_ref=target, send_sem=sent, recv_sem=received,
            device_id=device, device_id_type=MESH,
        )

    def z_copy(c, k):
        return remote(
            tok.at[c, pl.ds(0, own), :], tok.at[c, pl.ds(k * own, own), :],
            z_send.at[c, k - 1], z_recv.at[c, k - 1], z_peers[k - 1],
        )

    def near_copies(c):
        return (
            remote(tok.at[c, own_rows, :], tok.at[c, first_rows, :],
                   n_send.at[0, c], n_recv.at[0, c], first),
            remote(tok.at[c, own_rows, :], tok.at[c, second_rows, :],
                   n_send.at[1, c], n_recv.at[1, c], second),
        )

    def cross_copy(c):
        return remote(tok.at[c, first_rows, :], tok.at[c, cross_rows, :],
                      n_send.at[2, c], n_recv.at[2, c], second)

    def core_copy(j):
        return remote(acc.at[j, core_half, :], from_core.at[j], e_send.at[j], e_recv.at[j], core)

    low_copy = remote(low.at[core_half, :], low_from_core, e_send.at[tiles], e_recv.at[tiles], core)

    def hidden_copy(j):
        block = hid.at[my_half, pl.ds(pl.multiple_of(j * TILE, TILE), TILE)]
        return remote(block, block, h_send.at[j], h_recv.at[j], core)

    def sum_copy1(n):
        return remote(send1.at[n], recv1.at[n], r_send.at[0, n], r_recv.at[0, n], second)

    def sum_copy2(n):
        return remote(send2.at[n], recv2.at[n], r_send.at[1, n], r_recv.at[1, n], first)

    def sum_copy3(n, k):
        return remote(send3.at[n, k - 1], recv3.at[n, k - 1],
                      rz_send.at[n, k - 1], rz_recv.at[n, k - 1], z_peers[k - 1])

    barrier = pltpu.get_barrier_semaphore()
    peers = z_peers + [first, second, core]
    for peer in peers:
        pl.semaphore_signal(barrier, inc=1, device_id=peer, device_id_type=MESH)
    for c in range(SLOTS):
        for copy in weight_copies(c):
            copy.start()
    for copy in down_copies:
        copy.start()
    for c in range(STEPS):
        tok[c, 0:own, :] = tokens_ref[:, c * width:(c + 1) * width]
    pl.semaphore_wait(barrier, len(peers))
    for c in range(STEPS):
        for k in range(1, ZS):
            z_copy(c, k).start()

    @pl.loop(0, tiles)
    def _(j):
        acc[j] = jnp.zeros(acc.shape[1:], jnp.float32)

    low[...] = jnp.zeros_like(low)
    index_all[...] = jnp.broadcast_to(index_ref[...].astype(jnp.float32), (128, rows)).T
    for q in range(4):
        for k in range(ZS):
            source = pl.ds(pl.multiple_of(place(q, k) * own, own), own)
            index_rel[pl.ds(q * group + k * own, own), :] = index_all[source, :]

    def gather_step(t, carry):
        @pl.when(t < STEPS)
        def _():
            for k in range(1, ZS):
                z_copy(t, k).wait_recv()
            for copy in near_copies(t):
                copy.start()

        @pl.when((t >= GATHER_LAGS[0]) & (t < STEPS + GATHER_LAGS[0]))
        def _():
            near_copies(t - GATHER_LAGS[0])[0].wait_recv()
            cross_copy(t - GATHER_LAGS[0]).start()

        @pl.when(t >= GATHER_LAGS[1])
        def _():
            c = t - GATHER_LAGS[1]
            slot = c % SLOTS
            near_copies(c)[1].wait_recv()
            cross_copy(c).wait_recv()
            for copy in weight_copies(c):
                copy.wait()

            for j in range(tiles):
                part = pl.ds(j * TILE, TILE)
                acc[j, :, 0:TILE] += jnp.dot(
                    tok[c], wg[slot, :, part], preferred_element_type=jnp.float32
                )
                acc[j, :, TILE:2 * TILE] += jnp.dot(
                    tok[c], wu[slot, :, part], preferred_element_type=jnp.float32
                )

                @pl.when(c == STEPS - 1)
                def _():
                    core_copy(j).start()

            low[...] += lax.dot_general(
                tok[c], wa[slot], (((1,), (1,)), ((), ())), preferred_element_type=jnp.float32
            )

            @pl.when(c + SLOTS < STEPS)
            def _():
                for copy in weight_copies(c + SLOTS):
                    copy.start()

        return carry

    lax.fori_loop(0, STEPS + GATHER_LAGS[1], gather_step, 0)
    low_copy.start()

    @pl.loop(0, tiles)
    def _(j):
        core_copy(j).wait_recv()
        gate = acc[j, my_half, 0:TILE] + from_core[j, :, 0:TILE]
        up = acc[j, my_half, TILE:2 * TILE] + from_core[j, :, TILE:2 * TILE]
        value = gate / (1.0 + jnp.exp(-gate)) * up
        hid[my_half, pl.ds(pl.multiple_of(j * TILE, TILE), TILE)] = value.astype(jnp.bfloat16)
        hidden_copy(j).start()

    low_copy.wait_recv()
    adapters = store_ref.shape[1]
    ranks = low.shape[1]
    local = ranks // 64
    numbers = lax.broadcasted_iota(jnp.int32, (half, adapters), 1).astype(jnp.float32)
    store = jnp.broadcast_to(store_ref[...].astype(jnp.float32), (half, adapters))
    row_of = jnp.sum(
        jnp.where(index_rel[my_half, 0:adapters] == numbers, store, 0.0), axis=1, keepdims=True
    )
    held = lax.broadcasted_iota(jnp.int32, (half, ranks), 1) // 64 + tp * local
    low_sum = low[my_half, :] + low_from_core[...]
    low_sum = jnp.where(row_of == held.astype(jnp.float32), low_sum, 0.0)
    hid[my_half, pl.ds(tiles * TILE, TILE)] = low_sum.astype(jnp.bfloat16)
    hidden_copy(tiles).start()
    for copy in down_copies:
        copy.wait()

    @pl.loop(0, tiles + 1)
    def _(j):
        hidden_copy(j).wait_recv()

    def sum_step(t, carry):
        @pl.when(t < PARTS)
        def _():
            for i in range(columns // TILE):
                part = pl.ds(i * TILE, TILE)
                whole = pl.ds(pl.multiple_of(t * columns + i * TILE, TILE), TILE)
                base[t, :, part] = jnp.dot(
                    hid[...], wd[:, whole], preferred_element_type=jnp.float32
                )

            send1[t, 0:group, :] = base[t, second_rows, :].astype(jnp.bfloat16)
            send1[t, group:2 * group, :] = base[t, cross_rows, :].astype(jnp.bfloat16)
            sum_copy1(t).start()

        @pl.when((t >= SUM_LAGS[0]) & (t < PARTS + SUM_LAGS[0]))
        def _():
            n = t - SUM_LAGS[0]
            sum_copy1(n).wait_recv()
            send2[n] = (
                base[n, first_rows, :] + recv1[n, group:2 * group, :].astype(jnp.float32)
            ).astype(jnp.bfloat16)
            sum_copy2(n).start()
            base[n, own_rows, :] += recv1[n, 0:group, :].astype(jnp.float32)

        @pl.when((t >= SUM_LAGS[1]) & (t < PARTS + SUM_LAGS[1]))
        def _():
            n = t - SUM_LAGS[1]
            sum_copy2(n).wait_recv()
            total = base[n, own_rows, :] + recv2[n].astype(jnp.float32)
            base[n, pl.ds(0, own), :] = total[0:own]
            for k in range(1, ZS):
                send3[n, k - 1] = total[k * own:(k + 1) * own].astype(jnp.bfloat16)
                sum_copy3(n, k).start()

        @pl.when(t >= SUM_LAGS[2])
        def _():
            n = t - SUM_LAGS[2]
            total = base[n, pl.ds(0, own), :]
            for k in range(1, ZS):
                sum_copy3(n, k).wait_recv()
                total += recv3[n, k - 1].astype(jnp.float32)
            whole = pl.ds(pl.multiple_of(n * columns, columns), columns)
            out_ref[:, whole] = total.astype(jnp.bfloat16)

        return carry

    lax.fori_loop(0, PARTS + SUM_LAGS[2], sum_step, 0)

    @pl.loop(0, STEPS)
    def _(c):
        for k in range(1, ZS):
            z_copy(c, k).wait_send()
        for copy in near_copies(c):
            copy.wait_send()
        cross_copy(c).wait_send()

    @pl.loop(0, tiles)
    def _(j):
        core_copy(j).wait_send()

    low_copy.wait_send()

    @pl.loop(0, tiles + 1)
    def _(j):
        hidden_copy(j).wait_send()

    @pl.loop(0, PARTS)
    def _(n):
        sum_copy1(n).wait_send()
        sum_copy2(n).wait_send()
        for k in range(1, ZS):
            sum_copy3(n, k).wait_send()


def fused(
    tokens,
    gate_projection_weight,
    up_projection_weight,
    down_projection_weight,
    adapter_down_store,
    adapter_up_store,
    request_adapter_index,
    adapter_store_row,
):
    own, features = tokens.shape
    rows = request_adapter_index.shape[0]
    units = gate_projection_weight.shape[1]
    held, rank, _ = adapter_down_store.shape
    ranks = held * rank
    width = features // STEPS
    columns = features // PARTS
    tiles = units // TILE
    group = ZS * own
    bf16, f32 = jnp.bfloat16, jnp.float32
    dma = pltpu.SemaphoreType.DMA
    vmem = pl.BlockSpec(memory_space=pltpu.VMEM)
    hbm = pl.BlockSpec(memory_space=pl.ANY)
    return pl.pallas_call(
        layer_kernel,
        out_shape=jax.ShapeDtypeStruct((own, features), bf16),
        in_specs=[vmem, hbm, hbm, hbm, hbm, hbm, vmem, vmem],
        out_specs=vmem,
        scratch_shapes=[
            pltpu.VMEM((STEPS, rows, width), bf16),
            pltpu.VMEM((SLOTS, width, units), bf16),
            pltpu.VMEM((SLOTS, width, units), bf16),
            pltpu.VMEM((SLOTS, ranks, width), bf16),
            pltpu.VMEM((units + ranks, features), bf16),
            pltpu.VMEM((tiles, rows, 2 * TILE), f32),
            pltpu.VMEM((rows, ranks), f32),
            pltpu.VMEM((tiles, rows // 2, 2 * TILE), f32),
            pltpu.VMEM((rows // 2, ranks), f32),
            pltpu.VMEM((rows, units + ranks), bf16),
            pltpu.VMEM((PARTS, rows, columns), f32),
            pltpu.VMEM((PARTS, 2 * group, columns), bf16),
            pltpu.VMEM((PARTS, 2 * group, columns), bf16),
            pltpu.VMEM((PARTS, group, columns), bf16),
            pltpu.VMEM((PARTS, group, columns), bf16),
            pltpu.VMEM((PARTS, ZS - 1, own, columns), bf16),
            pltpu.VMEM((PARTS, ZS - 1, own, columns), bf16),
            pltpu.VMEM((rows, 128), f32),
            pltpu.VMEM((rows, 128), f32),
            dma((3, SLOTS)),
            dma((2,)),
            dma((STEPS, ZS - 1)),
            dma((STEPS, ZS - 1)),
            dma((3, STEPS)),
            dma((3, STEPS)),
            dma((tiles + 1,)),
            dma((tiles + 1,)),
            dma((tiles + 1,)),
            dma((tiles + 1,)),
            dma((2, PARTS)),
            dma((2, PARTS)),
            dma((PARTS, ZS - 1)),
            dma((PARTS, ZS - 1)),
        ],
        compiler_params=pltpu.CompilerParams(
            collective_id=0, has_side_effects=True, vmem_limit_bytes=61 * 1024 * 1024
        ),
    )(
        tokens,
        gate_projection_weight,
        up_projection_weight,
        down_projection_weight,
        adapter_down_store.reshape(ranks, features),
        adapter_up_store.reshape(ranks, features),
        request_adapter_index.reshape(1, rows),
        adapter_store_row.reshape(1, adapter_store_row.shape[0]),
    )


def solution(mesh):
    small = mesh.shape["tp"] == 16 and mesh.shape["rep"] == 1
    return jax.shard_map(
        fused if small else plain,
        mesh=mesh,
        in_specs=(
            P(("rep", "tp"), "sub"),
            P("sub", "tp"),
            P("sub", "tp"),
            P("tp", "sub"),
            P("tp", None, "sub"),
            P("tp", None, "sub"),
            P("rep"),
            P(),
        ),
        out_specs=P(("rep", "tp"), "sub"),
        check_vma=False,
    )
```
